32 devices in a mesh: src: 8 (over z, x), tgt: 4 (over y, core).
Axes of the slice: x: 2, y: 2, z: 4, core: 2. Of those that a mesh axis runs over, the one named last changes fastest.
Arguments:
- initial: bfloat16 [4096, 256], P(('src', 'tgt')), may hold values from -6 to 6
- stubborn: int32 [4096], P(('src', 'tgt')), may hold values from 0 to 255
- coupling: bfloat16 [256, 256], replicated, may hold values from -0.375 to 0.375
- tile_values: bfloat16 [8, 4, 144, 128, 128], P('src', 'tgt'), may hold values from -0.078125 to 0.078125
- tile_target: int32 [8, 4, 144], P('src', 'tgt'), may hold values from 0 to 3
- tile_source: int32 [8, 4, 144], P('src', 'tgt'), may hold values from 0 to 7, as said below
- tile_count: int32 [8, 4], P('src', 'tgt'), may hold values from 1 to 144, as said below
Outputs:
- opinions: bfloat16 [4096, 256], P(('src', 'tgt'))
The draws below stay inside these ranges and needn't reach their ends.
Inputs may be any that keep to these rules, and one draw needn't show every extreme that they name: Among the live slots k < tile_count of one block pair, tile_source does not fall as k rises; a source tile may hold several slots. `tile_count`: some block pair has all 144 slots live in every draw.
All inputs are finite; a program needn't handle non-finite values.
Results may differ from the reference program's by a relative error of at most 0.02.
Values may be sent and summed in bfloat16 or wider, within the bound.
No kernel may reach another device: no remote copies, remote signals or barrier semaphores. Data moves between devices by JAX's collectives and lax.ppermute only.
A program may use at most 64 MiB of HBM per device.

```python
import jax
import jax.numpy as jnp
from jax import lax

TOPICS = 256
TILE = 128
STEPS = 3
ROWS_DEV = 128
SLOTS = 144
USERS = 4096
SRC_TILES = 8
TGT_TILES = 4
N_SRC = 8
N_TGT = 4


def count_helper(key):
    base = jax.random.randint(jax.random.fold_in(key, 11), (N_SRC * N_TGT,), SLOTS // 6, SLOTS // 2 + 1)
    chosen = jax.random.randint(jax.random.fold_in(key, 12), (), 0, N_SRC * N_TGT)
    base = jnp.where(jnp.arange(N_SRC * N_TGT) == chosen, SLOTS, base)
    return base.reshape(N_SRC, N_TGT).astype(jnp.int32)


def draw_tile_count(key, part):
    return count_helper(key)


def draw_tile_source(key, part):
    counts = count_helper(key)
    raw = jax.random.randint(jax.random.fold_in(key, 13), (N_SRC, N_TGT, SLOTS), 0, SRC_TILES)
    active = jnp.arange(SLOTS)[None, None, :] < counts[:, :, None]
    keyed = jnp.where(active, raw, SRC_TILES)
    ordered = jnp.sort(keyed, axis=-1)
    return jnp.where(active, ordered, raw).astype(jnp.int32)


def plant(array, key, smallest, high):
    extent = array.shape
    index_at = [jax.random.randint(jax.random.fold_in(key, axis), (), 0, extent[axis]) for axis in range(len(extent))]
    array = array.at[tuple(index_at)].set(smallest)
    longest = extent.index(max(extent))
    index_at[longest] = (index_at[longest] + 1) % extent[longest]
    return array.at[tuple(index_at)].set(high)


def level_of(own_key, extent, shards, smallest, top_value):
    def one(position, blocks):
        steps = jax.random.uniform(jax.random.fold_in(jax.random.fold_in(own_key, 6), position), (blocks,), jnp.float32, smallest / len(shards), top_value / len(shards))
        return jnp.repeat(jnp.exp(steps), extent[position] // blocks).reshape((-1,) + (1,) * (len(extent) - position - 1))

    factor_of = one(*shards[0])
    for cut in shards[1:]:
        factor_of = factor_of * one(*cut)
    return factor_of


def noise(rng, dims, scale, limit, shards=(), held_as=jnp.bfloat16):
    drawn = jax.random.normal(rng, dims, jnp.float32) * scale
    if len(shards) > 0:
        drawn = level_of(rng, dims, shards, -0.22, 0.18) * drawn
    return jnp.clip(drawn, min=-limit, max=limit).astype(held_as)


def setup_inputs(seed: int = 0) -> dict:
    arg_keys = jax.random.split(jax.random.key(seed), 8)
    return {
        "initial": noise(arg_keys[0], (USERS, TOPICS), 1.0, 6.0, ((0, 32),)),
        "stubborn": plant(jax.random.randint(arg_keys[1], (USERS,), 0, 256), jax.random.fold_in(arg_keys[1], 1), 0, 255).astype(jnp.int32),
        "coupling": noise(arg_keys[2], (TOPICS, TOPICS), TOPICS ** -0.5, 0.375),
        "tile_values": noise(arg_keys[3], (N_SRC, N_TGT, SLOTS, TILE, TILE), (TILE * TILE * SLOTS // (3 * ROWS_DEV)) ** -0.5, 0.078125, ((0, 8), (1, 4))),
        "tile_target": plant(jax.random.randint(arg_keys[4], (N_SRC, N_TGT, SLOTS), 0, TGT_TILES), jax.random.fold_in(arg_keys[4], 1), 0, TGT_TILES - 1).astype(jnp.int32),
        "tile_source": draw_tile_source(jax.random.fold_in(arg_keys[7], 71), 0),
        "tile_count": draw_tile_count(jax.random.fold_in(arg_keys[7], 71), 0),
    }


def device_partial(blocked, tile_values, tile_target, tile_source, tile_count, row_group, column):
    per_block = ROWS_DEV // TILE
    sources_all = blocked[:, column].reshape(N_SRC * per_block, TILE, TOPICS)
    chosen = sources_all[tile_source[row_group, column]]
    active = (jnp.arange(SLOTS, dtype=jnp.int32) < tile_count[row_group, column]).astype(jnp.float32)
    contrib = jnp.einsum("kab,kbc->kac", tile_values[row_group, column].astype(jnp.float32), chosen.astype(jnp.float32))
    contrib = contrib * active[:, None, None]
    zeroed = jnp.zeros((N_TGT * per_block, TILE, TOPICS), jnp.float32)
    return zeroed.at[tile_target[row_group, column]].add(contrib)


def reference(initial, stubborn, coupling, tile_values, tile_target, tile_source, tile_count):
    per_block = ROWS_DEV // TILE
    openness = ((256.0 - stubborn.astype(jnp.float32)) / 256.0)[:, None]
    base_term = (1.0 - openness) * initial.astype(jnp.float32)
    opinion = initial
    for iteration in range(STEPS):
        blocked = opinion.reshape(N_SRC, N_TGT, per_block, TILE, TOPICS)

        def group_sum(row_group):
            def absorb(running, column):
                partial_value = device_partial(blocked, tile_values, tile_target, tile_source, tile_count, row_group, column)
                partial_value = lax.optimization_barrier(partial_value.astype(jnp.bfloat16))
                return running + partial_value.astype(jnp.float32), None

            zeroed = jnp.zeros((N_TGT * per_block, TILE, TOPICS), jnp.float32)
            total, unused = lax.scan(absorb, zeroed, jnp.arange(N_TGT, dtype=jnp.int32))
            return total

        summed = lax.map(group_sum, jnp.arange(N_SRC, dtype=jnp.int32)).reshape(USERS, TOPICS)
        influence = summed.astype(jnp.bfloat16)
        coupled = jnp.dot(influence, coupling, preferred_element_type=jnp.float32)
        opinion = (openness * coupled + base_term).astype(jnp.bfloat16)
    return opinion
```

```python
import functools

import jax
import jax.numpy as jnp
from jax import lax
from jax.experimental import pallas as pl
from jax.experimental.pallas import tpu as pltpu
from jax.sharding import PartitionSpec as P

STEPS = 3
ROW_TILES = 4
CHUNK = 16
BOTH = ("src", "tgt")


def densify_kernel(rows_ref, cols_ref, count_ref, tiles_ref, out_ref, total_ref):
    group, chunk = pl.program_id(0), pl.program_id(1)
    row_tiles, col_tiles, edge, _ = total_ref.shape

    @pl.when(chunk == 0)
    def _():
        total_ref[...] = jnp.zeros_like(total_ref)

    def absorb(k, carry):
        slot = chunk * CHUNK + k
        row = rows_ref[slot] - group * row_tiles

        @pl.when((row >= 0) & (row < row_tiles))
        def _():
            col = cols_ref[slot]
            total_ref[row, col] += tiles_ref[k].astype(jnp.float32)

        return carry

    live = jnp.clip(count_ref[0] - chunk * CHUNK, 0, CHUNK)
    lax.fori_loop(0, live, absorb, 0)

    @pl.when(chunk == pl.num_programs(1) - 1)
    def _():
        for i in range(row_tiles):
            for j in range(col_tiles):
                out_ref[i * edge:(i + 1) * edge, j * edge:(j + 1) * edge] = total_ref[i, j].astype(out_ref.dtype)


def densify(rows, cols, count, tiles, n_rows, n_cols):
    slots, edge, _ = tiles.shape
    row_tiles = min(ROW_TILES, n_rows)

    def pick(g, c, rows_ref, cols_ref, count_ref):
        return jnp.minimum(c, lax.div(count_ref[0] - 1, CHUNK)), 0, 0

    return pl.pallas_call(
        densify_kernel,
        out_shape=jax.ShapeDtypeStruct((n_rows * edge, n_cols * edge), jnp.bfloat16),
        grid_spec=pltpu.PrefetchScalarGridSpec(
            num_scalar_prefetch=3,
            grid=(n_rows // row_tiles, pl.cdiv(slots, CHUNK)),
            in_specs=[pl.BlockSpec((CHUNK, edge, edge), pick)],
            out_specs=pl.BlockSpec((row_tiles * edge, n_cols * edge), lambda g, c, *_: (g, 0)),
            scratch_shapes=[pltpu.VMEM((row_tiles, n_cols, edge, edge), jnp.float32)],
        ),
        compiler_params=pltpu.CompilerParams(vmem_limit_bytes=40 * 2**20),
        cost_estimate=pl.CostEstimate(flops=slots * edge * edge, bytes_accessed=2 * slots * edge * edge, transcendentals=0),
        name="densify",
    )(rows, cols, count, tiles)


def product_kernel(columns, weights_ref, *refs):
    *parts, out_ref = refs
    total = None
    for at, ref in zip(columns, parts):
        width = ref.shape[0]
        term = jnp.dot(weights_ref[:, at * 128:at * 128 + width], ref[...], preferred_element_type=jnp.float32)
        total = term if total is None else total + term
    out_ref[...] = total.astype(out_ref.dtype)


def product(weights, parts, columns):
    n_rows, n_cols = weights.shape
    topics = parts[0].shape[1]
    rows = min(n_rows, ROW_TILES * 128)
    return pl.pallas_call(
        functools.partial(product_kernel, columns),
        out_shape=jax.ShapeDtypeStruct((n_rows, topics), jnp.bfloat16),
        grid=(n_rows // rows,),
        in_specs=[pl.BlockSpec((rows, n_cols), lambda g: (g, 0))]
        + [pl.BlockSpec(p.shape, lambda g: (0, 0)) for p in parts],
        out_specs=pl.BlockSpec((rows, topics), lambda g: (g, 0)),
        compiler_params=pltpu.CompilerParams(vmem_limit_bytes=40 * 2**20),
        cost_estimate=pl.CostEstimate(flops=2 * n_rows * n_cols * topics, bytes_accessed=2 * n_rows * n_cols, transcendentals=0),
        name="product",
    )(weights, *parts)


def bits_of(n):
    assert n & (n - 1) == 0
    return [1 << i for i in range(n.bit_length() - 1)]


def shards(initial, stubborn, coupling, tile_values, tile_target, tile_source, tile_count):
    own_rows, topics = initial.shape
    n_src, n_tgt = lax.axis_size("src"), lax.axis_size("tgt")
    edge = tile_values.shape[-1]
    assert own_rows == edge
    s, t = lax.axis_index("src"), lax.axis_index("tgt")
    tgt_bits, src_bits = bits_of(n_tgt), bits_of(n_src)
    top, low = src_bits[-1], src_bits[:-1]

    def swap(value, src_mask, tgt_mask):
        mask = src_mask * n_tgt + tgt_mask
        return lax.ppermute(value, BOTH, [(d, d ^ mask) for d in range(n_src * n_tgt)])

    def spread(blocks):
        held = dict(blocks)
        pairs = [low[i:i + 2] for i in range(0, len(low), 2)]
        for pair in pairs:
            masks = [m for m in (pair if len(pair) == 1 else (pair[0], pair[1], pair[0] | pair[1]))]
            fresh = {}
            for block, value in held.items():
                for m in masks:
                    fresh[block | m] = swap(value, m, 0)
            held.update(fresh)
        return held

    relative = tile_target[0, 0] ^ t
    rows = sum(jnp.where(relative & b != 0, n_tgt // (2 * b), 0) for b in tgt_bits)
    cols = tile_source[0, 0] ^ s
    weights = densify(rows, cols, tile_count[0], tile_values[0, 0], n_tgt, n_src)

    openness = ((256.0 - stubborn.astype(jnp.float32)) / 256.0)[:, None]
    own = jnp.concatenate([initial, jnp.broadcast_to(openness.astype(jnp.bfloat16), (own_rows, 128))], axis=1)
    far = swap(own, top, 0)

    def update(influence, packed):
        start = packed[:, :topics].astype(jnp.float32)
        part = packed[:, topics:topics + 1].astype(jnp.float32)
        coupled = jnp.dot(influence, coupling, preferred_element_type=jnp.float32)
        return (part * coupled + (1.0 - part) * start).astype(jnp.bfloat16)

    def add(a, b):
        return (a.astype(jnp.float32) + b.astype(jnp.float32)).astype(jnp.bfloat16)

    held = spread({0: initial, top: far[:, :topics]})
    for step in range(STEPS):
        masks = sorted(held)
        terms = product(weights, [held[m] for m in masks], masks)
        for bit in tgt_bits[:-1]:
            half = terms.shape[0] // 2
            terms = add(terms[:half], swap(terms[half:], 0, bit))
        mine, other = terms[:own_rows], terms[own_rows:]
        last = tgt_bits[-1]
        near = update(add(mine, swap(other, 0, last)), own)
        if step == STEPS - 1:
            return near
        away = update(add(swap(mine, top, 0), swap(other, top, last)), far)
        held = spread({0: near, top: away})


def solution(mesh):
    in_specs = (
        P(("src", "tgt"), None),
        P(("src", "tgt")),
        P(),
        P("src", "tgt", None, None, None),
        P("src", "tgt", None),
        P("src", "tgt", None),
        P("src", "tgt"),
    )
    out_specs = P(("src", "tgt"), None)
    return jax.shard_map(shards, mesh=mesh, in_specs=in_specs, out_specs=out_specs, check_vma=False)
```

```python
import functools

import jax
import jax.numpy as jnp
from jax import lax
from jax.experimental import pallas as pl
from jax.experimental.pallas import tpu as pltpu
from jax.sharding import PartitionSpec as P

STEPS = 3
ROW_TILES = 4
CHUNK = 16
BOTH = ("src", "tgt")


def densify_kernel(target_ref, source_ref, count_ref, tiles_ref, out_ref, held_ref, total_ref, sems):
    group = pl.program_id(0)
    row_tiles, col_tiles, edge, _ = total_ref.shape
    slots = held_ref.shape[0]
    n_rows = pl.num_programs(0) * row_tiles
    s, t = lax.axis_index("src"), lax.axis_index("tgt")
    count = count_ref[0, 0]

    def copy(c):
        part = pl.ds(c * CHUNK, CHUNK)
        return pltpu.make_async_copy(tiles_ref.at[0, 0, part], held_ref.at[part], sems.at[c])

    for c in range(slots // CHUNK):
        pl.when((group == 0) & (c * CHUNK < count))(lambda c=c: copy(c).start())
    total_ref[...] = jnp.zeros_like(total_ref)

    def absorb(slot, carry):
        relative = target_ref[0, 0, slot] ^ t
        row = sum(jnp.where((relative & b) != 0, n_tgt // (2 * b), 0) for b in bits_of(n_tgt)) - group * row_tiles

        @pl.when((row >= 0) & (row < row_tiles))
        def _():
            col = source_ref[0, 0, slot] ^ s
            total_ref[row, col] += held_ref[slot].astype(jnp.float32)

        return carry

    n_tgt = lax.axis_size("tgt")
    for c in range(slots // CHUNK):
        pl.when((group == 0) & (c * CHUNK < count))(lambda c=c: copy(c).wait())
        lax.fori_loop(c * CHUNK, jnp.minimum(count, (c + 1) * CHUNK), absorb, 0)
    for i in range(row_tiles):
        for j in range(col_tiles):
            out_ref[i * edge:(i + 1) * edge, j * edge:(j + 1) * edge] = total_ref[i, j].astype(out_ref.dtype)


def densify(target, source, count, tiles, n_rows, n_cols):
    slots, edge = tiles.shape[2:4]
    assert slots % CHUNK == 0
    row_tiles = min(ROW_TILES, n_rows)
    scalars = pl.BlockSpec(memory_space=pltpu.SMEM)
    return pl.pallas_call(
        densify_kernel,
        out_shape=jax.ShapeDtypeStruct((n_rows * edge, n_cols * edge), jnp.bfloat16),
        grid=(n_rows // row_tiles,),
        in_specs=[scalars, scalars, scalars, pl.BlockSpec(memory_space=pltpu.HBM)],
        out_specs=pl.BlockSpec((row_tiles * edge, n_cols * edge), lambda g: (g, 0)),
        scratch_shapes=[
            pltpu.VMEM((slots, edge, edge), jnp.bfloat16),
            pltpu.VMEM((row_tiles, n_cols, edge, edge), jnp.float32),
            pltpu.SemaphoreType.DMA((slots // CHUNK,)),
        ],
        compiler_params=pltpu.CompilerParams(vmem_limit_bytes=52 * 2**20),
        cost_estimate=pl.CostEstimate(flops=slots * edge * edge, bytes_accessed=2 * slots * edge * edge, transcendentals=0),
        name="densify",
    )(target, source, count, tiles)


def product_kernel(columns, weights_ref, *refs):
    *parts, out_ref = refs
    total = None
    for group, ref in zip(columns, parts):
        for i, at in enumerate(group):
            block = ref[i * 128:(i + 1) * 128]
            term = jnp.dot(weights_ref[:, at * 128:(at + 1) * 128], block, preferred_element_type=jnp.float32)
            total = term if total is None else total + term
    out_ref[...] = total.astype(out_ref.dtype)


def product(weights, parts, columns):
    n_rows, n_cols = weights.shape
    topics = parts[0].shape[1]
    rows = min(n_rows, ROW_TILES * 128)
    return pl.pallas_call(
        functools.partial(product_kernel, columns),
        out_shape=jax.ShapeDtypeStruct((n_rows, topics), jnp.bfloat16),
        grid=(n_rows // rows,),
        in_specs=[pl.BlockSpec((rows, n_cols), lambda g: (g, 0))]
        + [pl.BlockSpec(p.shape, lambda g: (0, 0)) for p in parts],
        out_specs=pl.BlockSpec((rows, topics), lambda g: (g, 0)),
        compiler_params=pltpu.CompilerParams(vmem_limit_bytes=32 * 2**20),
        cost_estimate=pl.CostEstimate(flops=2 * n_rows * n_cols * topics, bytes_accessed=2 * n_rows * n_cols, transcendentals=0),
        name="product",
    )(weights, *parts)


def bits_of(n):
    assert n & (n - 1) == 0
    return [1 << i for i in range(n.bit_length() - 1)]


def shards(initial, stubborn, coupling, tile_values, tile_target, tile_source, tile_count):
    own_rows, topics = initial.shape
    n_src, n_tgt = lax.axis_size("src"), lax.axis_size("tgt")
    assert own_rows == tile_values.shape[-1]
    tgt_bits, src_bits = bits_of(n_tgt), bits_of(n_src)
    top, low = src_bits[-1], src_bits[:-1]

    def swap(value, src_mask, tgt_mask):
        mask = src_mask * n_tgt + tgt_mask
        return lax.ppermute(value, BOTH, [(d, d ^ mask) for d in range(n_src * n_tgt)])

    def spread(blocks):
        held = dict(blocks)
        for pair in [low[i:i + 2] for i in range(0, len(low), 2)]:
            masks = pair if len(pair) == 1 else (pair[0], pair[1], pair[0] | pair[1])
            held.update({tuple(k | m for k in ks): swap(value, m, 0) for ks, value in held.items() for m in masks})
        return held

    def gather(near):
        far = swap(near, top, 0)
        return spread({(0,): near}) | spread({(top,): far})

    weights = densify(tile_target, tile_source, tile_count, tile_values, n_tgt, n_src)
    openness = ((256.0 - stubborn.astype(jnp.float32)) / 256.0)[:, None]
    base = (1.0 - openness) * initial.astype(jnp.float32)

    def add(a, b):
        return (a.astype(jnp.float32) + b.astype(jnp.float32)).astype(jnp.bfloat16)

    opinion = initial
    for step in range(STEPS):
        held = gather(opinion)
        terms = product(weights, list(held.values()), list(held))
        for bit in tgt_bits:
            half = terms.shape[0] // 2
            terms = add(terms[:half], swap(terms[half:], 0, bit))
        coupled = jnp.dot(terms, coupling, preferred_element_type=jnp.float32)
        opinion = (openness * coupled + base).astype(jnp.bfloat16)
    return opinion


def solution(mesh):
    in_specs = (
        P(("src", "tgt"), None),
        P(("src", "tgt")),
        P(),
        P("src", "tgt", None, None, None),
        P("src", "tgt", None),
        P("src", "tgt", None),
        P("src", "tgt"),
    )
    out_specs = P(("src", "tgt"), None)
    return jax.shard_map(shards, mesh=mesh, in_specs=in_specs, out_specs=out_specs, check_vma=False)
```

```python
import functools

import jax
import jax.numpy as jnp
from jax import lax
from jax.experimental import pallas as pl
from jax.experimental.pallas import tpu as pltpu
from jax.sharding import PartitionSpec as P

STEPS = 3
ROW_TILES = 4
CHUNK = 16
UNROLL = 4
LOCAL = 32
BOTH = ("src", "tgt")


def densify_kernel(places_ref, tiles_ref, out_ref, held_ref, total_ref, sems):
    group = pl.program_id(0)
    slots, edge = held_ref.shape[:2]
    places = total_ref.shape[0] - 1
    columns = out_ref.shape[1] // edge
    count = places_ref[slots]

    def copy(c):
        part = pl.ds(c * CHUNK, CHUNK)
        return pltpu.make_async_copy(tiles_ref.at[0, 0, part], held_ref.at[part], sems.at[c])

    for c in range(slots // CHUNK):
        pl.when((group == 0) & (c * CHUNK < count))(lambda c=c: copy(c).start())
    total_ref[...] = jnp.zeros_like(total_ref)

    def absorb(c):
        pl.when(group == 0)(lambda: copy(c).wait())

        def some(k, carry):
            for i in range(UNROLL):
                slot = c * CHUNK + k * UNROLL + i
                place = places_ref[slot] - group * places
                place = jnp.where((place >= 0) & (place < places), place, places)
                total_ref[place] += held_ref[slot].astype(jnp.float32)
            return carry

        lax.fori_loop(0, CHUNK // UNROLL, some, 0)

    for c in range(slots // CHUNK):
        pl.when(c * CHUNK < count)(lambda c=c: absorb(c))
    for place in range(places):
        i, j = divmod(place, columns)
        out_ref[i * edge:(i + 1) * edge, j * edge:(j + 1) * edge] = total_ref[place].astype(out_ref.dtype)


def densify(places, tiles, n_rows, n_cols):
    slots, edge = tiles.shape[2:4]
    assert slots % CHUNK == 0
    row_tiles = min(ROW_TILES, n_rows)
    return pl.pallas_call(
        densify_kernel,
        out_shape=jax.ShapeDtypeStruct((n_rows * edge, n_cols * edge), jnp.bfloat16),
        grid=(n_rows // row_tiles,),
        in_specs=[pl.BlockSpec(memory_space=pltpu.SMEM), pl.BlockSpec(memory_space=pltpu.HBM)],
        out_specs=pl.BlockSpec((row_tiles * edge, n_cols * edge), lambda g: (g, 0)),
        scratch_shapes=[
            pltpu.VMEM((slots, edge, edge), jnp.bfloat16),
            pltpu.VMEM((row_tiles * n_cols + 1, edge, edge), jnp.float32),
            pltpu.SemaphoreType.DMA((slots // CHUNK,)),
        ],
        compiler_params=pltpu.CompilerParams(vmem_limit_bytes=52 * 2**20),
        cost_estimate=pl.CostEstimate(flops=slots * edge * edge, bytes_accessed=2 * slots * edge * edge, transcendentals=0),
        name="densify",
    )(places, tiles)


def early_kernel(weights_ref, *refs):
    *parts, total_ref = refs
    block = jnp.concatenate([ref[...] for ref in reversed(parts)], axis=0)
    for start, size in row_groups(total_ref.shape[0]):
        lhs = weights_ref[start:start + size, :block.shape[0]]
        total_ref[start:start + size] = jnp.dot(lhs, block, preferred_element_type=jnp.float32)


def late_kernel(quarters, begun, weights_ref, *refs):
    parts, outs = refs[begun:-len(quarters)], refs[-len(quarters):]
    block = jnp.concatenate([ref[...] for ref in reversed(parts)], axis=0)
    for quarter, out_ref in zip(quarters, outs):
        rows = out_ref.shape[0]
        for start, size in row_groups(rows):
            at = slice(quarter * rows + start, quarter * rows + start + size)
            lhs = weights_ref[at, weights_ref.shape[1] - block.shape[0]:]
            term = jnp.dot(lhs, block, preferred_element_type=jnp.float32)
            out_ref[start:start + size] = (refs[0][at] + term if begun else term).astype(out_ref.dtype)


def row_groups(rows):
    size = min(rows, ROW_TILES * 128)
    return [(start, size) for start in range(0, rows, size)]


def local(kernel, name, out_shapes, flops, *args):
    whole = pl.BlockSpec(memory_space=pltpu.VMEM)
    return pl.pallas_call(
        kernel,
        out_shape=out_shapes,
        in_specs=[whole] * len(args),
        out_specs=jax.tree.map(lambda _: whole, out_shapes),
        compiler_params=pltpu.CompilerParams(vmem_limit_bytes=LOCAL * 2**20),
        cost_estimate=pl.CostEstimate(flops=flops, bytes_accessed=0, transcendentals=0),
        name=name,
    )(*args)


def bits_of(n):
    assert n & (n - 1) == 0
    return [1 << i for i in range(n.bit_length() - 1)]


def shards(initial, stubborn, coupling, tile_values, tile_target, tile_source, tile_count):
    own_rows, topics = initial.shape
    n_src, n_tgt = lax.axis_size("src"), lax.axis_size("tgt")
    assert own_rows == tile_values.shape[-1]
    tgt_bits, src_bits = bits_of(n_tgt), bits_of(n_src)
    top, low = src_bits[-1], src_bits[:-1]

    def swap(value, src_mask, tgt_mask):
        mask = src_mask * n_tgt + tgt_mask
        return lax.ppermute(value, BOTH, [(d, d ^ mask) for d in range(n_src * n_tgt)])

    def spread(blocks):
        held = dict(blocks)
        for pair in [low[i:i + 2] for i in range(0, len(low), 2)]:
            masks = pair if len(pair) == 1 else (pair[0], pair[1], pair[0] | pair[1])
            held.update({k | m: swap(value, m, 0) for k, value in held.items() for m in masks})
        return held

    def gather(near):
        far = swap(near, top, 0)
        close, beyond = spread({0: near}), spread({top: far})
        beyond.pop(top)
        return [far] + [close[m] for m in sorted(close, reverse=True)], [beyond[m] for m in sorted(beyond, reverse=True)]

    row, column = tile_target[0, 0] ^ lax.axis_index("tgt"), tile_source[0, 0] ^ lax.axis_index("src")
    row = sum(jnp.where(row & b != 0, n_tgt // (2 * b), 0) for b in tgt_bits)
    live = jnp.arange(row.shape[0]) < tile_count[0, 0]
    places = jnp.where(live, row * n_src + column, n_tgt * n_src)
    weights = densify(jnp.concatenate([places, tile_count[0]]), tile_values, n_tgt, n_src)
    openness = ((256.0 - stubborn.astype(jnp.float32)) / 256.0)[:, None]
    base = (1.0 - openness) * initial.astype(jnp.float32)

    def add(a, b):
        return (a.astype(jnp.float32) + b.astype(jnp.float32)).astype(jnp.bfloat16)

    work = 2 * n_tgt * own_rows * own_rows * topics
    opinion = initial
    for step in range(STEPS):
        first, others = gather(opinion)
        begun = [] if step == 0 else [
            local(early_kernel, "early", jax.ShapeDtypeStruct((n_tgt * own_rows, topics), jnp.float32), work * len(first), weights, *first)
        ]
        late = begun + others if begun else others + first
        quarter = jax.ShapeDtypeStruct((n_tgt * own_rows // 4, topics), jnp.bfloat16)

        def finish(name, *quarters):
            kernel = functools.partial(late_kernel, quarters, len(begun))
            return local(kernel, name, [quarter] * len(quarters), work * len(late) * len(quarters) // 4, weights, *late)

        (sent,) = finish("late_first", 3)
        received = swap(sent, 0, tgt_bits[0])
        kept, mine, sent = finish("late_rest", 1, 0, 2)
        other = swap(add(kept, received), 0, tgt_bits[1])
        terms = add(add(mine, swap(sent, 0, tgt_bits[0])), other)
        for bit in tgt_bits[2:]:
            half = terms.shape[0] // 2
            terms = add(terms[:half], swap(terms[half:], 0, bit))
        coupled = jnp.dot(terms, coupling, preferred_element_type=jnp.float32)
        opinion = (openness * coupled + base).astype(jnp.bfloat16)
    return opinion


def solution(mesh):
    in_specs = (
        P(("src", "tgt"), None),
        P(("src", "tgt")),
        P(),
        P("src", "tgt", None, None, None),
        P("src", "tgt", None),
        P("src", "tgt", None),
        P("src", "tgt"),
    )
    out_specs = P(("src", "tgt"), None)
    return jax.shard_map(shards, mesh=mesh, in_specs=in_specs, out_specs=out_specs, check_vma=False)
```

```python
import functools

import jax
import jax.numpy as jnp
from jax import lax
from jax.experimental import pallas as pl
from jax.experimental.pallas import tpu as pltpu
from jax.sharding import PartitionSpec as P

STEPS = 3
ROW_TILES = 4
CHUNK = 16
UNROLL = 4
LOCAL = 32
BOTH = ("src", "tgt")


def densify_kernel(places_ref, tiles_ref, out_ref, held_ref, total_ref, sems):
    group = pl.program_id(0)
    slots, edge = held_ref.shape[:2]
    places = total_ref.shape[0] - 1
    columns = out_ref.shape[1] // edge
    count = places_ref[slots]

    def copy(c):
        part = pl.ds(c * CHUNK, CHUNK)
        return pltpu.make_async_copy(tiles_ref.at[0, 0, part], held_ref.at[part], sems.at[c])

    for c in range(slots // CHUNK):
        pl.when((group == 0) & (c * CHUNK < count))(lambda c=c: copy(c).start())
    total_ref[...] = jnp.zeros_like(total_ref)

    def absorb(c):
        pl.when(group == 0)(lambda: copy(c).wait())

        def some(k, carry):
            for i in range(UNROLL):
                slot = c * CHUNK + k * UNROLL + i
                place = places_ref[slot] - group * places
                place = jnp.where((place >= 0) & (place < places), place, places)
                total_ref[place] += held_ref[slot].astype(jnp.float32)
            return carry

        lax.fori_loop(0, CHUNK // UNROLL, some, 0)

    for c in range(slots // CHUNK):
        pl.when(c * CHUNK < count)(lambda c=c: absorb(c))
    for place in range(places):
        i, j = divmod(place, columns)
        out_ref[i * edge:(i + 1) * edge, j * edge:(j + 1) * edge] = total_ref[place].astype(out_ref.dtype)


def densify(places, tiles, n_rows, n_cols):
    slots, edge = tiles.shape[2:4]
    assert slots % CHUNK == 0
    row_tiles = min(ROW_TILES, n_rows)
    return pl.pallas_call(
        densify_kernel,
        out_shape=jax.ShapeDtypeStruct((n_rows * edge, n_cols * edge), jnp.bfloat16),
        grid=(n_rows // row_tiles,),
        in_specs=[pl.BlockSpec(memory_space=pltpu.SMEM), pl.BlockSpec(memory_space=pltpu.HBM)],
        out_specs=pl.BlockSpec((row_tiles * edge, n_cols * edge), lambda g: (g, 0)),
        scratch_shapes=[
            pltpu.VMEM((slots, edge, edge), jnp.bfloat16),
            pltpu.VMEM((row_tiles * n_cols + 1, edge, edge), jnp.float32),
            pltpu.SemaphoreType.DMA((slots // CHUNK,)),
        ],
        compiler_params=pltpu.CompilerParams(vmem_limit_bytes=52 * 2**20),
        cost_estimate=pl.CostEstimate(flops=slots * edge * edge, bytes_accessed=2 * slots * edge * edge, transcendentals=0),
        name="densify",
    )(places, tiles)


def early_kernel(weights_ref, *refs):
    *parts, total_ref = refs
    block = jnp.concatenate([ref[...] for ref in parts], axis=0)
    for start, size in row_groups(total_ref.shape[0]):
        lhs = weights_ref[start:start + size, :block.shape[0]]
        total_ref[start:start + size] = jnp.dot(lhs, block, preferred_element_type=jnp.float32)


def late_kernel(quarters, begun, weights_ref, *refs):
    parts, outs = refs[begun:-len(quarters)], refs[-len(quarters):]
    block = jnp.concatenate([ref[...] for ref in parts], axis=0)
    for quarter, out_ref in zip(quarters, outs):
        rows = out_ref.shape[0]
        for start, size in row_groups(rows):
            at = slice(quarter * rows + start, quarter * rows + start + size)
            lhs = weights_ref[at, weights_ref.shape[1] - block.shape[0]:]
            term = jnp.dot(lhs, block, preferred_element_type=jnp.float32)
            out_ref[start:start + size] = (refs[0][at] + term if begun else term).astype(out_ref.dtype)


def row_groups(rows):
    size = min(rows, ROW_TILES * 128)
    return [(start, size) for start in range(0, rows, size)]


def local(kernel, name, out_shapes, flops, *args):
    whole = pl.BlockSpec(memory_space=pltpu.VMEM)
    return pl.pallas_call(
        kernel,
        out_shape=out_shapes,
        in_specs=[whole] * len(args),
        out_specs=jax.tree.map(lambda _: whole, out_shapes),
        compiler_params=pltpu.CompilerParams(vmem_limit_bytes=LOCAL * 2**20),
        cost_estimate=pl.CostEstimate(flops=flops, bytes_accessed=0, transcendentals=0),
        name=name,
    )(*args)


def bits_of(n):
    assert n & (n - 1) == 0
    return [1 << i for i in range(n.bit_length() - 1)]


def shards(initial, stubborn, coupling, tile_values, tile_target, tile_source, tile_count):
    own_rows, topics = initial.shape
    n_src, n_tgt = lax.axis_size("src"), lax.axis_size("tgt")
    assert own_rows == tile_values.shape[-1]
    tgt_bits, src_bits = bits_of(n_tgt), bits_of(n_src)
    top, low = src_bits[-1], src_bits[:-1]

    def swap(value, src_mask, tgt_mask):
        mask = src_mask * n_tgt + tgt_mask
        return lax.ppermute(value, BOTH, [(d, d ^ mask) for d in range(n_src * n_tgt)])

    def spread(blocks):
        held = dict(blocks)
        for pair in [low[i:i + 2] for i in range(0, len(low), 2)]:
            masks = pair if len(pair) == 1 else (pair[0], pair[1], pair[0] | pair[1])
            held.update({k | m: swap(value, m, 0) for k, value in held.items() for m in masks})
        return held

    def gather(near):
        across = tgt_bits[0]
        there = swap(near, top, across)
        far = swap(there, 0, across)
        close, beyond = spread({0: near}), {top: far}
        for i in range(0, len(low), 2):
            pair = low[i:i + 2]
            masks = pair if len(pair) == 1 else (pair[0], pair[1], pair[0] | pair[1])
            if i == 0:
                beyond |= {top | m: swap(there, m, across) for m in masks}
            else:
                beyond |= {k | m: swap(value, m, 0) for k, value in beyond.items() for m in masks}
        return [close[m] for m in sorted(close)], [beyond[m] for m in sorted(beyond)]

    row, column = tile_target[0, 0] ^ lax.axis_index("tgt"), tile_source[0, 0] ^ lax.axis_index("src")
    row = sum(jnp.where(row & b != 0, n_tgt // (2 * b), 0) for b in tgt_bits)
    live = jnp.arange(row.shape[0]) < tile_count[0, 0]
    places = jnp.where(live, row * n_src + column, n_tgt * n_src)
    weights = densify(jnp.concatenate([places, tile_count[0]]), tile_values, n_tgt, n_src)
    openness = ((256.0 - stubborn.astype(jnp.float32)) / 256.0)[:, None]
    base = (1.0 - openness) * initial.astype(jnp.float32)

    def add(a, b):
        return (a.astype(jnp.float32) + b.astype(jnp.float32)).astype(jnp.bfloat16)

    work = 2 * n_tgt * own_rows * own_rows * topics
    opinion = initial
    for step in range(STEPS):
        first, others = gather(opinion)
        begun = [] if step == 0 else [
            local(early_kernel, "early", jax.ShapeDtypeStruct((n_tgt * own_rows, topics), jnp.float32), work * len(first), weights, *first)
        ]
        late = begun + others if begun else first + others
        quarter = jax.ShapeDtypeStruct((n_tgt * own_rows // 4, topics), jnp.bfloat16)

        def finish(name, *quarters):
            kernel = functools.partial(late_kernel, quarters, len(begun))
            return local(kernel, name, [quarter] * len(quarters), work * len(late) * len(quarters) // 4, weights, *late)

        (sent,) = finish("late_first", 3)
        received = swap(sent, 0, tgt_bits[0])
        kept, mine, sent = finish("late_rest", 1, 0, 2)
        other = swap(add(kept, received), 0, tgt_bits[1])
        terms = add(add(mine, swap(sent, 0, tgt_bits[0])), other)
        for bit in tgt_bits[2:]:
            half = terms.shape[0] // 2
            terms = add(terms[:half], swap(terms[half:], 0, bit))
        coupled = jnp.dot(terms, coupling, preferred_element_type=jnp.float32)
        opinion = (openness * coupled + base).astype(jnp.bfloat16)
    return opinion


def solution(mesh):
    in_specs = (
        P(("src", "tgt"), None),
        P(("src", "tgt")),
        P(),
        P("src", "tgt", None, None, None),
        P("src", "tgt", None),
        P("src", "tgt", None),
        P("src", "tgt"),
    )
    out_specs = P(("src", "tgt"), None)
    return jax.shard_map(shards, mesh=mesh, in_specs=in_specs, out_specs=out_specs, check_vma=False)
```

```python
import functools

import jax
import jax.numpy as jnp
from jax import lax
from jax.experimental import pallas as pl
from jax.experimental.pallas import tpu as pltpu
from jax.sharding import PartitionSpec as P

STEPS = 3
ROW_TILES = 4
UNROLL = 4
LOCAL = 32
BOTH = ("src", "tgt")


def densify_kernel(places_ref, tiles_ref, out_ref, total_ref):
    group = pl.program_id(0)
    slots, edge = tiles_ref.shape[2:4]
    places = total_ref.shape[0] - 1
    columns = out_ref.shape[1] // edge
    count = places_ref[slots]
    total_ref[...] = jnp.zeros_like(total_ref)

    def some(k, carry):
        for i in range(UNROLL):
            slot = k * UNROLL + i
            place = places_ref[slot] - group * places
            place = jnp.where((place >= 0) & (place < places), place, places)
            total_ref[place] += tiles_ref[0, 0, slot].astype(jnp.float32)
        return carry

    lax.fori_loop(0, pl.cdiv(count, UNROLL), some, 0)
    for place in range(places):
        i, j = divmod(place, columns)
        out_ref[i * edge:(i + 1) * edge, j * edge:(j + 1) * edge] = total_ref[place].astype(out_ref.dtype)


def densify(places, tiles, n_rows, n_cols):
    slots, edge = tiles.shape[2:4]
    assert slots % UNROLL == 0
    row_tiles = min(ROW_TILES, n_rows)
    return pl.pallas_call(
        densify_kernel,
        out_shape=jax.ShapeDtypeStruct((n_rows * edge, n_cols * edge), jnp.bfloat16),
        grid=(n_rows // row_tiles,),
        in_specs=[pl.BlockSpec(memory_space=pltpu.SMEM), pl.BlockSpec(memory_space=pltpu.VMEM)],
        out_specs=pl.BlockSpec((row_tiles * edge, n_cols * edge), lambda g: (g, 0)),
        scratch_shapes=[
            pltpu.VMEM((row_tiles * n_cols + 1, edge, edge), jnp.float32),
        ],
        compiler_params=pltpu.CompilerParams(vmem_limit_bytes=24 * 2**20),
        cost_estimate=pl.CostEstimate(flops=slots * edge * edge, bytes_accessed=2 * slots * edge * edge, transcendentals=0),
        name="densify",
    )(places, tiles)


def early_kernel(weights_ref, *refs):
    *parts, total_ref = refs
    block = jnp.concatenate([ref[...] for ref in parts], axis=0)
    for start, size in row_groups(total_ref.shape[0]):
        lhs = weights_ref[start:start + size, :block.shape[0]]
        total_ref[start:start + size] = jnp.dot(lhs, block, preferred_element_type=jnp.float32)


def late_kernel(quarters, begun, weights_ref, *refs):
    parts, outs = refs[begun:-len(quarters)], refs[-len(quarters):]
    block = jnp.concatenate([ref[...] for ref in parts], axis=0)
    for quarter, out_ref in zip(quarters, outs):
        rows = out_ref.shape[0]
        for start, size in row_groups(rows):
            at = slice(quarter * rows + start, quarter * rows + start + size)
            lhs = weights_ref[at, weights_ref.shape[1] - block.shape[0]:]
            term = jnp.dot(lhs, block, preferred_element_type=jnp.float32)
            out_ref[start:start + size] = (refs[0][at] + term if begun else term).astype(out_ref.dtype)


def place_kernel(past, count_ref, place_ref, out_ref):
    slot = lax.broadcasted_iota(jnp.int32, place_ref.shape, 1)
    out_ref[...] = jnp.where(slot < count_ref[...], place_ref[...], past)


def row_groups(rows):
    size = min(rows, ROW_TILES * 128)
    return [(start, size) for start in range(0, rows, size)]


def local(kernel, name, out_shapes, flops, *args):
    whole = pl.BlockSpec(memory_space=pltpu.VMEM)
    return pl.pallas_call(
        kernel,
        out_shape=out_shapes,
        in_specs=[whole] * len(args),
        out_specs=jax.tree.map(lambda _: whole, out_shapes),
        compiler_params=pltpu.CompilerParams(vmem_limit_bytes=LOCAL * 2**20),
        cost_estimate=pl.CostEstimate(flops=flops, bytes_accessed=0, transcendentals=0),
        name=name,
    )(*args)


def bits_of(n):
    assert n & (n - 1) == 0
    return [1 << i for i in range(n.bit_length() - 1)]


def shards(initial, stubborn, coupling, tile_values, tile_target, tile_source, tile_count):
    own_rows, topics = initial.shape
    n_src, n_tgt = lax.axis_size("src"), lax.axis_size("tgt")
    assert own_rows == tile_values.shape[-1]
    tgt_bits, src_bits = bits_of(n_tgt), bits_of(n_src)
    top, low = src_bits[-1], src_bits[:-1]

    def swap(value, src_mask, tgt_mask):
        mask = src_mask * n_tgt + tgt_mask
        return lax.ppermute(value, BOTH, [(d, d ^ mask) for d in range(n_src * n_tgt)])

    def spread(blocks):
        held = dict(blocks)
        for pair in [low[i:i + 2] for i in range(0, len(low), 2)]:
            masks = pair if len(pair) == 1 else (pair[0], pair[1], pair[0] | pair[1])
            held.update({k | m: swap(value, m, 0) for k, value in held.items() for m in masks})
        return held

    def gather(near):
        across = tgt_bits[0]
        there = swap(near, top, across)
        far = swap(there, 0, across)
        close, beyond = spread({0: near}), {top: far}
        for i in range(0, len(low), 2):
            pair = low[i:i + 2]
            masks = pair if len(pair) == 1 else (pair[0], pair[1], pair[0] | pair[1])
            if i == 0:
                beyond |= {top | m: swap(there, m, across) for m in masks}
            else:
                beyond |= {k | m: swap(value, m, 0) for k, value in beyond.items() for m in masks}
        return [close[m] for m in sorted(close)], [beyond[m] for m in sorted(beyond)]

    row, column = tile_target[0] ^ lax.axis_index("tgt"), tile_source[0] ^ lax.axis_index("src")
    row = sum(jnp.where(row & b != 0, n_tgt // (2 * b), 0) for b in tgt_bits)
    places = local(
        functools.partial(place_kernel, n_tgt * n_src), "places", jax.ShapeDtypeStruct(row.shape, jnp.int32), 2 * 10**10, tile_count, row * n_src + column
    )
    weights = densify(jnp.concatenate([places[0], tile_count[0]]), tile_values, n_tgt, n_src)
    openness = ((256.0 - stubborn.astype(jnp.float32)) / 256.0)[:, None]
    base = (1.0 - openness) * initial.astype(jnp.float32)

    def add(a, b):
        return (a.astype(jnp.float32) + b.astype(jnp.float32)).astype(jnp.bfloat16)

    work = 2 * n_tgt * own_rows * own_rows * topics
    opinion = initial
    for step in range(STEPS):
        first, others = gather(opinion)
        begun = [] if step == 0 else [
            local(early_kernel, "early", jax.ShapeDtypeStruct((n_tgt * own_rows, topics), jnp.float32), work * len(first), weights, *first)
        ]
        late = begun + others if begun else first + others
        quarter = jax.ShapeDtypeStruct((n_tgt * own_rows // 4, topics), jnp.bfloat16)

        def finish(name, *quarters):
            kernel = functools.partial(late_kernel, quarters, len(begun))
            return local(kernel, name, [quarter] * len(quarters), work * len(late) * len(quarters) // 4, weights, *late)

        (sent,) = finish("late_first", 3)
        received = swap(sent, 0, tgt_bits[0])
        kept, mine, sent = finish("late_rest", 1, 0, 2)
        other = swap(add(kept, received), 0, tgt_bits[1])
        terms = add(add(mine, swap(sent, 0, tgt_bits[0])), other)
        for bit in tgt_bits[2:]:
            half = terms.shape[0] // 2
            terms = add(terms[:half], swap(terms[half:], 0, bit))
        coupled = jnp.dot(terms, coupling, preferred_element_type=jnp.float32)
        opinion = (openness * coupled + base).astype(jnp.bfloat16)
    return opinion


def solution(mesh):
    in_specs = (
        P(("src", "tgt"), None),
        P(("src", "tgt")),
        P(),
        P("src", "tgt", None, None, None),
        P("src", "tgt", None),
        P("src", "tgt", None),
        P("src", "tgt"),
    )
    out_specs = P(("src", "tgt"), None)
    return jax.shard_map(shards, mesh=mesh, in_specs=in_specs, out_specs=out_specs, check_vma=False)
```

```python
import functools

import jax
import jax.numpy as jnp
from jax import lax
from jax.experimental import pallas as pl
from jax.experimental.pallas import tpu as pltpu
from jax.sharding import PartitionSpec as P

STEPS = 3
ROW_TILES = 4
UNROLL = 4
LOCAL = 32
BOTH = ("src", "tgt")


def densify_kernel(places_ref, tiles_ref, out_ref, total_ref):
    group = pl.program_id(0)
    slots, edge = tiles_ref.shape[2:4]
    places = total_ref.shape[0] - 1
    columns = out_ref.shape[1] // edge
    count = places_ref[slots]
    total_ref[...] = jnp.zeros_like(total_ref)

    def some(k, carry):
        for i in range(UNROLL):
            slot = k * UNROLL + i
            place = places_ref[slot] - group * places
            place = jnp.where((place >= 0) & (place < places), place, places)
            total_ref[place] += tiles_ref[0, 0, slot].astype(jnp.float32)
        return carry

    lax.fori_loop(0, pl.cdiv(count, UNROLL), some, 0)
    for place in range(places):
        i, j = divmod(place, columns)
        out_ref[i * edge:(i + 1) * edge, j * edge:(j + 1) * edge] = total_ref[place].astype(out_ref.dtype)


def densify(places, tiles, n_rows, n_cols):
    slots, edge = tiles.shape[2:4]
    assert slots % UNROLL == 0
    row_tiles = min(ROW_TILES, n_rows)
    return pl.pallas_call(
        densify_kernel,
        out_shape=jax.ShapeDtypeStruct((n_rows * edge, n_cols * edge), jnp.bfloat16),
        grid=(n_rows // row_tiles,),
        in_specs=[pl.BlockSpec(memory_space=pltpu.SMEM), pl.BlockSpec(memory_space=pltpu.VMEM)],
        out_specs=pl.BlockSpec((row_tiles * edge, n_cols * edge), lambda g: (g, 0)),
        scratch_shapes=[
            pltpu.VMEM((row_tiles * n_cols + 1, edge, edge), jnp.float32),
        ],
        compiler_params=pltpu.CompilerParams(vmem_limit_bytes=24 * 2**20),
        cost_estimate=pl.CostEstimate(flops=slots * edge * edge, bytes_accessed=2 * slots * edge * edge, transcendentals=0),
        name="densify",
    )(places, tiles)


def early_kernel(weights_ref, *refs):
    *parts, total_ref = refs
    block = jnp.concatenate([ref[...] for ref in parts], axis=0)
    for start, size in row_groups(total_ref.shape[0]):
        lhs = weights_ref[start:start + size, :block.shape[0]]
        total_ref[start:start + size] = jnp.dot(lhs, block, preferred_element_type=jnp.float32)


def late_kernel(quarters, begun, weights_ref, *refs):
    parts, outs = refs[begun:-len(quarters)], refs[-len(quarters):]
    block = jnp.concatenate([ref[...] for ref in parts], axis=0)
    for quarter, out_ref in zip(quarters, outs):
        rows = out_ref.shape[0]
        for start, size in row_groups(rows):
            at = slice(quarter * rows + start, quarter * rows + start + size)
            lhs = weights_ref[at, weights_ref.shape[1] - block.shape[0]:]
            term = jnp.dot(lhs, block, preferred_element_type=jnp.float32)
            out_ref[start:start + size] = (refs[0][at] + term if begun else term).astype(out_ref.dtype)


def update_kernel(coupling_ref, openness_ref, initial_ref, *refs):
    terms, out_ref = refs[:-1], refs[-1]
    influence = sum(ref[...].astype(jnp.float32) for ref in terms).astype(jnp.bfloat16)
    coupled = jnp.dot(influence, coupling_ref[...], preferred_element_type=jnp.float32)
    openness, initial = openness_ref[...], initial_ref[...].astype(jnp.float32)
    out_ref[...] = (openness * coupled + (1.0 - openness) * initial).astype(out_ref.dtype)


def place_kernel(past, count_ref, place_ref, out_ref):
    slot = lax.broadcasted_iota(jnp.int32, place_ref.shape, 1)
    out_ref[...] = jnp.where(slot < count_ref[...], place_ref[...], past)


def row_groups(rows):
    size = min(rows, ROW_TILES * 128)
    return [(start, size) for start in range(0, rows, size)]


def local(kernel, name, out_shapes, flops, *args):
    whole = pl.BlockSpec(memory_space=pltpu.VMEM)
    return pl.pallas_call(
        kernel,
        out_shape=out_shapes,
        in_specs=[whole] * len(args),
        out_specs=jax.tree.map(lambda _: whole, out_shapes),
        compiler_params=pltpu.CompilerParams(vmem_limit_bytes=LOCAL * 2**20),
        cost_estimate=pl.CostEstimate(flops=flops, bytes_accessed=0, transcendentals=0),
        name=name,
    )(*args)


def bits_of(n):
    assert n & (n - 1) == 0
    return [1 << i for i in range(n.bit_length() - 1)]


def shards(initial, stubborn, coupling, tile_values, tile_target, tile_source, tile_count):
    own_rows, topics = initial.shape
    n_src, n_tgt = lax.axis_size("src"), lax.axis_size("tgt")
    assert own_rows == tile_values.shape[-1]
    tgt_bits, src_bits = bits_of(n_tgt), bits_of(n_src)
    top, low = src_bits[-1], src_bits[:-1]

    def swap(value, src_mask, tgt_mask):
        mask = src_mask * n_tgt + tgt_mask
        return lax.ppermute(value, BOTH, [(d, d ^ mask) for d in range(n_src * n_tgt)])

    def spread(blocks):
        held = dict(blocks)
        for pair in [low[i:i + 2] for i in range(0, len(low), 2)]:
            masks = pair if len(pair) == 1 else (pair[0], pair[1], pair[0] | pair[1])
            held.update({k | m: swap(value, m, 0) for k, value in held.items() for m in masks})
        return held

    def gather(near):
        across = tgt_bits[0]
        there = swap(near, top, across)
        far = swap(there, 0, across)
        close, beyond = spread({0: near}), {top: far}
        for i in range(0, len(low), 2):
            pair = low[i:i + 2]
            masks = pair if len(pair) == 1 else (pair[0], pair[1], pair[0] | pair[1])
            if i == 0:
                beyond |= {top | m: swap(there, m, across) for m in masks}
            else:
                beyond |= {k | m: swap(value, m, 0) for k, value in beyond.items() for m in masks}
        return [close[m] for m in sorted(close)], [beyond[m] for m in sorted(beyond)]

    row, column = tile_target[0] ^ lax.axis_index("tgt"), tile_source[0] ^ lax.axis_index("src")
    row = sum(jnp.where(row & b != 0, n_tgt // (2 * b), 0) for b in tgt_bits)
    places = local(
        functools.partial(place_kernel, n_tgt * n_src), "places", jax.ShapeDtypeStruct(row.shape, jnp.int32), 2 * 10**10, tile_count, row * n_src + column
    )
    weights = densify(jnp.concatenate([places[0], tile_count[0]]), tile_values, n_tgt, n_src)
    openness = ((256.0 - stubborn.astype(jnp.float32)) / 256.0)[:, None]
    base = (1.0 - openness) * initial.astype(jnp.float32)

    def add(a, b):
        return (a.astype(jnp.float32) + b.astype(jnp.float32)).astype(jnp.bfloat16)

    work = 2 * n_tgt * own_rows * own_rows * topics
    opinion = initial
    for step in range(STEPS):
        first, others = gather(opinion)
        begun = [] if step == 0 else [
            local(early_kernel, "early", jax.ShapeDtypeStruct((n_tgt * own_rows, topics), jnp.float32), work * len(first), weights, *first)
        ]
        late = begun + others if begun else first + others
        quarter = jax.ShapeDtypeStruct((n_tgt * own_rows // 4, topics), jnp.bfloat16)

        def finish(name, *quarters):
            kernel = functools.partial(late_kernel, quarters, len(begun))
            return local(kernel, name, [quarter] * len(quarters), work * len(late) * len(quarters) // 4, weights, *late)

        (sent,) = finish("late_first", 3)
        received = swap(sent, 0, tgt_bits[0])
        kept, mine, sent = finish("late_rest", 1, 0, 2)
        terms = [mine, swap(sent, 0, tgt_bits[0]), swap(add(kept, received), 0, tgt_bits[1])]
        for bit in tgt_bits[2:]:
            total = functools.reduce(add, terms)
            half = total.shape[0] // 2
            terms = [total[:half], swap(total[half:], 0, bit)]
        if step < STEPS - 1:
            opinion = local(update_kernel, "update", jax.ShapeDtypeStruct(initial.shape, jnp.bfloat16), 2 * own_rows * topics**2, coupling, openness, initial, *terms)
    coupled = jnp.dot(functools.reduce(add, terms), coupling, preferred_element_type=jnp.float32)
    opinion = (openness * coupled + base).astype(jnp.bfloat16)
    return opinion


def solution(mesh):
    in_specs = (
        P(("src", "tgt"), None),
        P(("src", "tgt")),
        P(),
        P("src", "tgt", None, None, None),
        P("src", "tgt", None),
        P("src", "tgt", None),
        P("src", "tgt"),
    )
    out_specs = P(("src", "tgt"), None)
    return jax.shard_map(shards, mesh=mesh, in_specs=in_specs, out_specs=out_specs, check_vma=False)
```

```python
import functools

import jax
import jax.numpy as jnp
from jax import lax
from jax.experimental import pallas as pl
from jax.experimental.pallas import tpu as pltpu
from jax.sharding import PartitionSpec as P

STEPS = 3
ROW_TILES = 4
UNROLL = 4
LOCAL = 32
BOTH = ("src", "tgt")


def densify_kernel(places_ref, tiles_ref, out_ref, total_ref):
    group = pl.program_id(0)
    slots, edge = tiles_ref.shape[2:4]
    places = total_ref.shape[0] - 1
    columns = out_ref.shape[1] // edge
    count = places_ref[slots]
    total_ref[...] = jnp.zeros_like(total_ref)

    def some(k, carry):
        for i in range(UNROLL):
            slot = k * UNROLL + i
            place = places_ref[slot] - group * places
            place = jnp.where((slot < count) & (place >= 0) & (place < places), place, places)
            total_ref[place] += tiles_ref[0, 0, slot].astype(jnp.float32)
        return carry

    lax.fori_loop(0, pl.cdiv(count, UNROLL), some, 0)
    for place in range(places):
        i, j = divmod(place, columns)
        out_ref[i * edge:(i + 1) * edge, j * edge:(j + 1) * edge] = total_ref[place].astype(out_ref.dtype)


def densify(places, tiles, n_rows, n_cols):
    slots, edge = tiles.shape[2:4]
    assert slots % UNROLL == 0
    row_tiles = min(ROW_TILES, n_rows)
    return pl.pallas_call(
        densify_kernel,
        out_shape=jax.ShapeDtypeStruct((n_rows * edge, n_cols * edge), jnp.bfloat16),
        grid=(n_rows // row_tiles,),
        in_specs=[pl.BlockSpec(memory_space=pltpu.SMEM), pl.BlockSpec(memory_space=pltpu.VMEM)],
        out_specs=pl.BlockSpec((row_tiles * edge, n_cols * edge), lambda g: (g, 0)),
        scratch_shapes=[
            pltpu.VMEM((row_tiles * n_cols + 1, edge, edge), jnp.float32),
        ],
        compiler_params=pltpu.CompilerParams(vmem_limit_bytes=24 * 2**20),
        cost_estimate=pl.CostEstimate(flops=slots * edge * edge, bytes_accessed=2 * slots * edge * edge, transcendentals=0),
        name="densify",
    )(places, tiles)


def early_kernel(weights_ref, *refs):
    *parts, total_ref = refs
    block = jnp.concatenate([ref[...] for ref in parts], axis=0)
    for start, size in row_groups(total_ref.shape[0]):
        lhs = weights_ref[start:start + size, :block.shape[0]]
        total_ref[start:start + size] = jnp.dot(lhs, block, preferred_element_type=jnp.float32)


def late_kernel(quarters, begun, weights_ref, *refs):
    parts, outs = refs[begun:-len(quarters)], refs[-len(quarters):]
    block = jnp.concatenate([ref[...] for ref in parts], axis=0)
    for quarter, out_ref in zip(quarters, outs):
        rows = out_ref.shape[0]
        for start, size in row_groups(rows):
            at = slice(quarter * rows + start, quarter * rows + start + size)
            lhs = weights_ref[at, weights_ref.shape[1] - block.shape[0]:]
            term = jnp.dot(lhs, block, preferred_element_type=jnp.float32)
            out_ref[start:start + size] = (refs[0][at] + term if begun else term).astype(out_ref.dtype)


def update_kernel(coupling_ref, openness_ref, initial_ref, *refs):
    terms, out_ref = refs[:-1], refs[-1]
    influence = sum(ref[...].astype(jnp.float32) for ref in terms).astype(jnp.bfloat16)
    coupled = jnp.dot(influence, coupling_ref[...], preferred_element_type=jnp.float32)
    openness, initial = openness_ref[...], initial_ref[...].astype(jnp.float32)
    out_ref[...] = (openness * coupled + (1.0 - openness) * initial).astype(out_ref.dtype)


def place_kernel(row_ref, column_ref, out_ref):
    out_ref[...] = row_ref[...] + column_ref[...]


def row_groups(rows):
    size = min(rows, ROW_TILES * 128)
    return [(start, size) for start in range(0, rows, size)]


def local(kernel, name, out_shapes, flops, *args):
    whole = pl.BlockSpec(memory_space=pltpu.VMEM)
    return pl.pallas_call(
        kernel,
        out_shape=out_shapes,
        in_specs=[whole] * len(args),
        out_specs=jax.tree.map(lambda _: whole, out_shapes),
        compiler_params=pltpu.CompilerParams(vmem_limit_bytes=LOCAL * 2**20),
        cost_estimate=pl.CostEstimate(flops=flops, bytes_accessed=0, transcendentals=0),
        name=name,
    )(*args)


def bits_of(n):
    assert n & (n - 1) == 0
    return [1 << i for i in range(n.bit_length() - 1)]


def shards(initial, stubborn, coupling, tile_values, tile_target, tile_source, tile_count):
    own_rows, topics = initial.shape
    n_src, n_tgt = lax.axis_size("src"), lax.axis_size("tgt")
    assert own_rows == tile_values.shape[-1]
    tgt_bits, src_bits = bits_of(n_tgt), bits_of(n_src)
    top, low = src_bits[-1], src_bits[:-1]

    def swap(value, src_mask, tgt_mask):
        mask = src_mask * n_tgt + tgt_mask
        return lax.ppermute(value, BOTH, [(d, d ^ mask) for d in range(n_src * n_tgt)])

    def spread(blocks):
        held = dict(blocks)
        for pair in [low[i:i + 2] for i in range(0, len(low), 2)]:
            masks = pair if len(pair) == 1 else (pair[0], pair[1], pair[0] | pair[1])
            held.update({k | m: swap(value, m, 0) for k, value in held.items() for m in masks})
        return held

    def gather(near):
        across = tgt_bits[0]
        there = swap(near, top, across)
        far = swap(there, 0, across)
        close, beyond = spread({0: near}), {top: far}
        for i in range(0, len(low), 2):
            pair = low[i:i + 2]
            masks = pair if len(pair) == 1 else (pair[0], pair[1], pair[0] | pair[1])
            if i == 0:
                beyond |= {top | m: swap(there, m, across) for m in masks}
            else:
                beyond |= {k | m: swap(value, m, 0) for k, value in beyond.items() for m in masks}
        return [close[m] for m in sorted(close)], [beyond[m] for m in sorted(beyond)]

    row, column = tile_target[0] ^ lax.axis_index("tgt"), tile_source[0] ^ lax.axis_index("src")
    row = sum(jnp.where(row & b != 0, n_src * n_tgt // (2 * b), 0) for b in tgt_bits)
    places = local(
        place_kernel, "places", jax.ShapeDtypeStruct(row.shape, jnp.int32), 2 * 10**10, row, column
    )
    weights = densify(jnp.concatenate([places[0], tile_count[0]]), tile_values, n_tgt, n_src)
    openness = ((256.0 - stubborn.astype(jnp.float32)) / 256.0)[:, None]
    base = (1.0 - openness) * initial.astype(jnp.float32)

    def add(a, b):
        return (a.astype(jnp.float32) + b.astype(jnp.float32)).astype(jnp.bfloat16)

    work = 2 * n_tgt * own_rows * own_rows * topics
    opinion = initial
    for step in range(STEPS):
        first, others = gather(opinion)
        begun = [] if step == 0 else [
            local(early_kernel, "early", jax.ShapeDtypeStruct((n_tgt * own_rows, topics), jnp.float32), work * len(first), weights, *first)
        ]
        late = begun + others if begun else first + others
        quarter = jax.ShapeDtypeStruct((n_tgt * own_rows // 4, topics), jnp.bfloat16)

        def finish(name, *quarters):
            kernel = functools.partial(late_kernel, quarters, len(begun))
            return local(kernel, name, [quarter] * len(quarters), work * len(late) * len(quarters) // 4, weights, *late)

        (sent,) = finish("late_first", 3)
        received = swap(sent, 0, tgt_bits[0])
        kept, mine, sent = finish("late_rest", 1, 0, 2)
        terms = [mine, swap(sent, 0, tgt_bits[0]), swap(add(kept, received), 0, tgt_bits[1])]
        for bit in tgt_bits[2:]:
            total = functools.reduce(add, terms)
            half = total.shape[0] // 2
            terms = [total[:half], swap(total[half:], 0, bit)]
        if step < STEPS - 1:
            opinion = local(update_kernel, "update", jax.ShapeDtypeStruct(initial.shape, jnp.bfloat16), 2 * own_rows * topics**2, coupling, openness, initial, *terms)
    coupled = jnp.dot(functools.reduce(add, terms), coupling, preferred_element_type=jnp.float32)
    opinion = (openness * coupled + base).astype(jnp.bfloat16)
    return opinion


def solution(mesh):
    in_specs = (
        P(("src", "tgt"), None),
        P(("src", "tgt")),
        P(),
        P("src", "tgt", None, None, None),
        P("src", "tgt", None),
        P("src", "tgt", None),
        P("src", "tgt"),
    )
    out_specs = P(("src", "tgt"), None)
    return jax.shard_map(shards, mesh=mesh, in_specs=in_specs, out_specs=out_specs, check_vma=False)
```

```python
import functools

import jax
import jax.numpy as jnp
from jax import lax
from jax.experimental import pallas as pl
from jax.experimental.pallas import tpu as pltpu
from jax.sharding import PartitionSpec as P

STEPS = 3
ROW_TILES = 4
UNROLL = 4
LOCAL = 32
BOTH = ("src", "tgt")


def densify_kernel(places_ref, tiles_ref, out_ref, total_ref):
    group = pl.program_id(0)
    slots, edge = tiles_ref.shape[2:4]
    places = total_ref.shape[0] - 1
    columns = out_ref.shape[1] // edge
    count = places_ref[slots]
    total_ref[...] = jnp.zeros_like(total_ref)

    def some(k, carry):
        for i in range(UNROLL):
            slot = k * UNROLL + i
            place = places_ref[slot] - group * places
            place = jnp.where((place >= 0) & (place < places), place, places)
            total_ref[place] += tiles_ref[0, 0, slot].astype(jnp.float32)
        return carry

    lax.fori_loop(0, pl.cdiv(count, UNROLL), some, 0)
    for place in range(places):
        i, j = divmod(place, columns)
        out_ref[i * edge:(i + 1) * edge, j * edge:(j + 1) * edge] = total_ref[place].astype(out_ref.dtype)


def densify(places, tiles, n_rows, n_cols):
    slots, edge = tiles.shape[2:4]
    assert slots % UNROLL == 0
    row_tiles = min(ROW_TILES, n_rows)
    return pl.pallas_call(
        densify_kernel,
        out_shape=jax.ShapeDtypeStruct((n_rows * edge, n_cols * edge), jnp.bfloat16),
        grid=(n_rows // row_tiles,),
        in_specs=[pl.BlockSpec(memory_space=pltpu.SMEM), pl.BlockSpec(memory_space=pltpu.VMEM)],
        out_specs=pl.BlockSpec((row_tiles * edge, n_cols * edge), lambda g: (g, 0)),
        scratch_shapes=[
            pltpu.VMEM((row_tiles * n_cols + 1, edge, edge), jnp.float32),
        ],
        compiler_params=pltpu.CompilerParams(vmem_limit_bytes=24 * 2**20),
        cost_estimate=pl.CostEstimate(flops=slots * edge * edge, bytes_accessed=2 * slots * edge * edge, transcendentals=0),
        name="densify",
    )(places, tiles)


def early_kernel(weights_ref, *refs):
    *parts, total_ref = refs
    block = jnp.concatenate([ref[...] for ref in parts], axis=0)
    for start, size in row_groups(total_ref.shape[0]):
        lhs = weights_ref[start:start + size, :block.shape[0]]
        total_ref[start:start + size] = jnp.dot(lhs, block, preferred_element_type=jnp.float32)


def late_kernel(quarters, begun, weights_ref, *refs):
    parts, outs = refs[begun:-len(quarters)], refs[-len(quarters):]
    block = jnp.concatenate([ref[...] for ref in parts], axis=0)
    for quarter, out_ref in zip(quarters, outs):
        rows = out_ref.shape[0]
        for start, size in row_groups(rows):
            at = slice(quarter * rows + start, quarter * rows + start + size)
            lhs = weights_ref[at, weights_ref.shape[1] - block.shape[0]:]
            term = jnp.dot(lhs, block, preferred_element_type=jnp.float32)
            out_ref[start:start + size] = (refs[0][at] + term if begun else term).astype(out_ref.dtype)


def update_kernel(coupling_ref, openness_ref, initial_ref, *refs):
    terms, out_ref = refs[:-1], refs[-1]
    influence = sum(ref[...].astype(jnp.float32) for ref in terms).astype(jnp.bfloat16)
    coupled = jnp.dot(influence, coupling_ref[...], preferred_element_type=jnp.float32)
    openness, initial = openness_ref[...], initial_ref[...].astype(jnp.float32)
    out_ref[...] = (openness * coupled + (1.0 - openness) * initial).astype(out_ref.dtype)


def last_kernel(coupling_ref, openness_ref, initial_ref, *refs):
    terms, (out_ref, held_ref, sems) = refs[:-3], refs[-3:]
    rows = held_ref.shape[0] // 2
    copies = []
    for i in range(2):
        at = pl.ds(i * rows, rows)
        update_kernel(coupling_ref, openness_ref.at[at], initial_ref.at[at], *(ref.at[at] for ref in terms), held_ref.at[at])
        copies.append(pltpu.make_async_copy(held_ref.at[at], out_ref.at[at], sems.at[i]))
        copies[i].start()
    for copy in copies:
        copy.wait()


def place_kernel(past, count_ref, place_ref, out_ref):
    slot = lax.broadcasted_iota(jnp.int32, place_ref.shape, 1)
    out_ref[...] = jnp.where(slot < count_ref[...], place_ref[...], past)


def row_groups(rows):
    size = min(rows, ROW_TILES * 128)
    return [(start, size) for start in range(0, rows, size)]


def local(kernel, name, out_shapes, flops, *args):
    whole = pl.BlockSpec(memory_space=pltpu.VMEM)
    return pl.pallas_call(
        kernel,
        out_shape=out_shapes,
        in_specs=[whole] * len(args),
        out_specs=jax.tree.map(lambda _: whole, out_shapes),
        compiler_params=pltpu.CompilerParams(vmem_limit_bytes=LOCAL * 2**20),
        cost_estimate=pl.CostEstimate(flops=flops, bytes_accessed=0, transcendentals=0),
        name=name,
    )(*args)


def bits_of(n):
    assert n & (n - 1) == 0
    return [1 << i for i in range(n.bit_length() - 1)]


def shards(initial, stubborn, coupling, tile_values, tile_target, tile_source, tile_count):
    own_rows, topics = initial.shape
    n_src, n_tgt = lax.axis_size("src"), lax.axis_size("tgt")
    assert own_rows == tile_values.shape[-1]
    tgt_bits, src_bits = bits_of(n_tgt), bits_of(n_src)
    top, low = src_bits[-1], src_bits[:-1]

    def swap(value, src_mask, tgt_mask):
        mask = src_mask * n_tgt + tgt_mask
        return lax.ppermute(value, BOTH, [(d, d ^ mask) for d in range(n_src * n_tgt)])

    def spread(blocks):
        held = dict(blocks)
        for pair in [low[i:i + 2] for i in range(0, len(low), 2)]:
            masks = pair if len(pair) == 1 else (pair[0], pair[1], pair[0] | pair[1])
            held.update({k | m: swap(value, m, 0) for k, value in held.items() for m in masks})
        return held

    def gather(near):
        across = tgt_bits[0]
        there = swap(near, top, across)
        far = swap(there, 0, across)
        close, beyond = spread({0: near}), {top: far}
        for i in range(0, len(low), 2):
            pair = low[i:i + 2]
            masks = pair if len(pair) == 1 else (pair[0], pair[1], pair[0] | pair[1])
            if i == 0:
                beyond |= {top | m: swap(there, m, across) for m in masks}
            else:
                beyond |= {k | m: swap(value, m, 0) for k, value in beyond.items() for m in masks}
        return [close[m] for m in sorted(close)], [beyond[m] for m in sorted(beyond)]

    row, column = tile_target[0] ^ lax.axis_index("tgt"), tile_source[0] ^ lax.axis_index("src")
    row = sum(jnp.where(row & b != 0, n_tgt // (2 * b), 0) for b in tgt_bits)
    places = local(
        functools.partial(place_kernel, n_tgt * n_src), "places", jax.ShapeDtypeStruct(row.shape, jnp.int32), 2 * 10**10, tile_count, row * n_src + column
    )
    weights = densify(jnp.concatenate([places[0], tile_count[0]]), tile_values, n_tgt, n_src)
    openness = ((256.0 - stubborn.astype(jnp.float32)) / 256.0)[:, None]

    def add(a, b):
        return (a.astype(jnp.float32) + b.astype(jnp.float32)).astype(jnp.bfloat16)

    work = 2 * n_tgt * own_rows * own_rows * topics
    opinion = initial
    for step in range(STEPS):
        first, others = gather(opinion)
        begun = [] if step == 0 else [
            local(early_kernel, "early", jax.ShapeDtypeStruct((n_tgt * own_rows, topics), jnp.float32), work * len(first), weights, *first)
        ]
        late = begun + others if begun else first + others
        quarter = jax.ShapeDtypeStruct((n_tgt * own_rows // 4, topics), jnp.bfloat16)

        def finish(name, *quarters):
            kernel = functools.partial(late_kernel, quarters, len(begun))
            return local(kernel, name, [quarter] * len(quarters), work * len(late) * len(quarters) // 4, weights, *late)

        (sent,) = finish("late_first", 3)
        received = swap(sent, 0, tgt_bits[0])
        kept, mine, sent = finish("late_rest", 1, 0, 2)
        terms = [mine, swap(sent, 0, tgt_bits[0]), swap(add(kept, received), 0, tgt_bits[1])]
        for bit in tgt_bits[2:]:
            total = functools.reduce(add, terms)
            half = total.shape[0] // 2
            terms = [total[:half], swap(total[half:], 0, bit)]
        if step < STEPS - 1:
            opinion = local(update_kernel, "update", jax.ShapeDtypeStruct(initial.shape, jnp.bfloat16), 2 * own_rows * topics**2, coupling, openness, initial, *terms)
    whole = pl.BlockSpec(memory_space=pltpu.VMEM)
    return pl.pallas_call(
        last_kernel,
        out_shape=jax.ShapeDtypeStruct(initial.shape, jnp.bfloat16),
        in_specs=[whole] * (3 + len(terms)),
        out_specs=pl.BlockSpec(memory_space=pltpu.HBM),
        scratch_shapes=[pltpu.VMEM(initial.shape, jnp.bfloat16), pltpu.SemaphoreType.DMA((2,))],
        compiler_params=pltpu.CompilerParams(vmem_limit_bytes=LOCAL * 2**20),
        cost_estimate=pl.CostEstimate(flops=2 * own_rows * topics**2, bytes_accessed=2 * own_rows * topics, transcendentals=0),
        name="last",
    )(coupling, openness, initial, *terms)


def solution(mesh):
    in_specs = (
        P(("src", "tgt"), None),
        P(("src", "tgt")),
        P(),
        P("src", "tgt", None, None, None),
        P("src", "tgt", None),
        P("src", "tgt", None),
        P("src", "tgt"),
    )
    out_specs = P(("src", "tgt"), None)
    return jax.shard_map(shards, mesh=mesh, in_specs=in_specs, out_specs=out_specs, check_vma=False)
```
